32 devices in a mesh: chan: 16 (over z, x, core), tm: 2 (over y).
Axes of the slice: x: 2, y: 2, z: 4, core: 2. Of those that a mesh axis runs over, the one named last changes fastest.
Arguments:
- raw_strain: bfloat16 [2048, 16384], P('chan', 'tm'), may hold values from -6 to 6
- fir_taps: bfloat16 [64], replicated, may hold values from -0.75 to 0.75
- sources: int32 [2, 8], replicated, may hold values from 0 to 2047, as said below
Outputs:
- correlation: float32 [2, 8, 257, 2048], P(None, 'tm', None, 'chan')
The draws below stay inside these ranges and needn't reach their ends.
Inputs may be any that keep to these rules, and one draw needn't show every extreme that they name: `sources`: the 16 entries are distinct channel indices; the first and the last channel are always among them.
All inputs are finite; a program needn't handle non-finite values.
Results may differ from the reference program's by a relative error of at most 0.0037.
Values may be sent and summed in bfloat16 or wider, within the bound.
A program may use at most 64 MiB of HBM per device.

```python
import math
import jax
import jax.numpy as jnp
from jax import lax

CH_DEV = 128
TAPS = 64
DECIM = 4
HALF_WIN = 32
LAGS = 257
HALF_LAG = 128
STEPS = 2
PER_STEP = 8
SOURCES = 16
CHANNELS = 2048
DEC = 4096
RAW = 16384
N_CHAN = 16


def draw_sources(key, part):
    first_key = jax.random.fold_in(key, 11)
    second_key = jax.random.fold_in(key, 23)
    middle = jax.random.permutation(first_key, CHANNELS - 2)[:STEPS * PER_STEP - 2] + 1
    ends = jnp.array([0, CHANNELS - 1], jnp.int32)
    entries = jnp.concatenate([ends, middle.astype(jnp.int32)])
    order = jax.random.permutation(second_key, STEPS * PER_STEP)
    return entries[order].reshape(STEPS, PER_STEP).astype(jnp.int32)


def block_levels(own_key, extent, split, least, largest):
    loudness, own = 1.0, jax.random.fold_in(own_key, 6)
    for axis_at, blocks in split:
        draws = jnp.exp(jax.random.uniform(jax.random.fold_in(own, axis_at), (blocks,), jnp.float32, least / len(split), largest / len(split)))
        loudness = loudness * jnp.repeat(draws, extent[axis_at] // blocks).reshape([-1 if axis == axis_at else 1 for axis in range(len(extent))])
    return loudness


def normal_values(own_key, extent, width, limit, shards=(), held_as=jnp.bfloat16):
    factor_of = block_levels(own_key, extent, shards, -0.22, 0.18) if shards else 1.0
    values = jax.random.normal(own_key, extent, jnp.float32) * width * factor_of
    return jnp.minimum(jnp.maximum(values, -limit), limit).astype(held_as)


def setup_inputs(seed: int = 0) -> dict:
    streams_of = jax.random.split(jax.random.key(seed), 4)
    raw_strain = normal_values(streams_of[0], (CHANNELS, RAW), 1.0, 6.0, ((0, 16), (1, 2)))
    fir_taps = normal_values(streams_of[1], (TAPS,), TAPS ** -0.5, 0.75)
    sources = draw_sources(jax.random.fold_in(streams_of[3], 71), 0)
    return dict(raw_strain=raw_strain, fir_taps=fir_taps, sources=sources)


def reference(raw_strain, fir_taps, sources):
    taps_wide = fir_taps.astype(jnp.float32)

    def clean(block):
        padded = jnp.pad(block.astype(jnp.float32), ((0, 0), (TAPS, 0)))
        decimated = jnp.zeros((block.shape[0], DEC), jnp.float32)
        for tap_index in range(TAPS):
            begin = TAPS - tap_index
            decimated = decimated + taps_wide[tap_index] * padded[:, begin:begin + DECIM * DEC:DECIM]
        magnitude = jnp.pad(jnp.abs(decimated), ((0, 0), (HALF_WIN, HALF_WIN)))
        window_total = jnp.zeros((block.shape[0], DEC), jnp.float32)
        for offset in range(2 * HALF_WIN + 1):
            window_total = window_total + magnitude[:, offset:offset + DEC]
        level = window_total / (2 * HALF_WIN + 1) + 1e-05
        return (decimated / level).astype(jnp.bfloat16)
    white = lax.map(clean, raw_strain.reshape(N_CHAN, CH_DEV, RAW)).reshape(CHANNELS, DEC)
    traces = white[sources.reshape(-1).astype(jnp.int32)].astype(jnp.float32)
    length = DEC + LAGS - 1
    trace_spectra = jnp.conj(jnp.fft.rfft(traces, n=length, axis=-1))

    def correlate(block):
        spectra = jnp.fft.rfft(block.astype(jnp.float32), n=length, axis=-1)
        circular = jnp.fft.irfft(trace_spectra[:, None, :] * spectra[None, :, :], n=length, axis=-1)
        lagged = jnp.concatenate([circular[..., length - HALF_LAG:], circular[..., :HALF_LAG + 1]], axis=-1)
        return jnp.transpose(lagged, (0, 2, 1))
    blocks = lax.map(correlate, white.reshape(N_CHAN, CH_DEV, DEC))
    result = jnp.transpose(blocks, (1, 2, 0, 3)).reshape(SOURCES, LAGS, CHANNELS)
    result = result / math.sqrt(DEC)
    return result.reshape(STEPS, PER_STEP, LAGS, CHANNELS).astype(jnp.float32)
```

```python
import functools
import math

import jax
import jax.numpy as jnp
from jax import lax
from jax.experimental import pallas as pl
from jax.experimental.pallas import tpu as pltpu
from jax.sharding import PartitionSpec as P

TAPS = 64
DECIM = 4
HALF_WIN = 32
LAGS = 257
HALF_LAG = 128
STEPS = 2
W = 128
SLAB = 8
PIECES = 4
LEFT = 256
RIGHT = 128
MESH = pl.DeviceIdType.MESH


def nt(a, b):
    return lax.dot_general(
        a, b, (((1,), (1,)), ((), ())), preferred_element_type=jnp.float32
    )


def aligned(x):
    return pl.multiple_of(x, W)


def kernel(
    C, T, scale,
    raw_ref, taps_ref, src_ref, out_ref,
    x_ref, dec_ref, hi_ref, lo_ref, white_ref, send1, recv1, recv2, gref, acc_ref,
    load_sem, halo_send, halo_recv, s1_sem, r1_sem, s2_sem, r2_sem, own_sem, bulk_send, bulk_recv,
):
    c = lax.axis_index("chan")
    t = lax.axis_index("tm")
    N = C * T
    rows, raw_len = raw_ref.shape
    dec_len = raw_len // DECIM
    nb = dec_len // W
    per_dev = (T * nb) // C
    half = nb // per_dev
    step_len = src_ref.shape[1] // T
    ns = STEPS * step_len
    me = c * T + t

    barrier = pltpu.get_barrier_semaphore()

    def greet(d, _):
        other = lax.rem(me + d, N)
        pl.semaphore_signal(
            barrier, inc=1, device_id=(other // T, lax.rem(other, T)), device_id_type=MESH
        )
        return 0

    lax.fori_loop(1, N, greet, 0)

    seg = raw_len // PIECES
    loads = []
    for i in range(PIECES):
        load = pltpu.make_async_copy(
            raw_ref.at[:, pl.ds(i * seg, seg)],
            x_ref.at[:, pl.ds(LEFT + i * seg, seg)],
            load_sem.at[i],
        )
        load.start()
        loads.append(load)

    taps = jnp.broadcast_to(taps_ref[...], (16, TAPS))
    place = lax.broadcasted_iota(jnp.int32, (TAPS, W), 1) == lax.rem(
        W - lax.broadcasted_iota(jnp.int32, (TAPS, W), 0), W
    )
    base = jnp.dot(
        taps, place.astype(jnp.float32).astype(jnp.bfloat16), preferred_element_type=jnp.float32
    )
    rolled = pltpu.roll(
        jnp.broadcast_to(base[0:1, :], (W, W)), 0, 1, stride=DECIM, stride_axis=0
    )
    row_id = lax.broadcasted_iota(jnp.int32, (W, W), 0)
    lane_id = lax.broadcasted_iota(jnp.int32, (W, W), 1)
    fts = []
    for jc in range(DECIM + 1):
        k = DECIM * row_id + W - W * jc - lane_id
        fts.append(jnp.where((k >= 0) & (k < W), rolled, 0.0).astype(jnp.bfloat16))
    ft = jnp.concatenate(fts, axis=1)

    pl.semaphore_wait(barrier, N - 1)

    to_right = pltpu.make_async_remote_copy(
        src_ref=raw_ref.at[:, pl.ds(raw_len - LEFT, LEFT)],
        dst_ref=x_ref.at[:, pl.ds(0, LEFT)],
        send_sem=halo_send.at[0], recv_sem=halo_recv.at[0],
        device_id=(c, lax.rem(t + 1, T)), device_id_type=MESH,
    )
    to_left = pltpu.make_async_remote_copy(
        src_ref=raw_ref.at[:, pl.ds(0, RIGHT)],
        dst_ref=x_ref.at[:, pl.ds(LEFT + raw_len, RIGHT)],
        send_sem=halo_send.at[1], recv_sem=halo_recv.at[1],
        device_id=(c, lax.rem(t + T - 1, T)), device_id_type=MESH,
    )

    @pl.when(t < T - 1)
    def _():
        to_right.start()

    @pl.when(t > 0)
    def _():
        to_left.start()

    @pl.when(t == 0)
    def _():
        x_ref[:, 0:LEFT] = jnp.zeros((rows, LEFT), jnp.bfloat16)

    @pl.when(t == T - 1)
    def _():
        x_ref[:, LEFT + raw_len:] = jnp.zeros((rows, RIGHT), jnp.bfloat16)

    total = T * dec_len
    white_ref[:, 0:W] = jnp.zeros((rows, W), jnp.bfloat16)
    white_ref[:, W + total:] = jnp.zeros((rows, W), jnp.bfloat16)

    def put_mag(b, d):
        mag = jnp.abs(d)
        hi = mag.astype(jnp.bfloat16)
        hi_ref[:, (b + 1) * W:(b + 2) * W] = hi
        lo_ref[:, (b + 1) * W:(b + 2) * W] = (mag - hi.astype(jnp.float32)).astype(jnp.bfloat16)

    def chunk(b):
        begin = LEFT - W + b * DECIM * W
        d = nt(x_ref[:, begin:begin + (DECIM + 1) * W], ft)
        dec_ref[:, b * W:(b + 1) * W] = d
        put_mag(b, d)

    loaded = 0
    for b in range(1, nb):
        while loaded * seg < min((b + 1) * DECIM * W, raw_len):
            loads[loaded].wait()
            loaded += 1
        chunk(b)

    @pl.when(t > 0)
    def _():
        to_right.wait_recv()

    @pl.when(t < T - 1)
    def _():
        to_left.wait_recv()

    chunk(0)
    before = nt(x_ref[:, 0:LEFT], ft[:, 3 * W:5 * W])
    keep = (t > 0) & (lax.broadcasted_iota(jnp.int32, (rows, W), 1) >= W - HALF_WIN)
    put_mag(-1, jnp.where(keep, before, 0.0))
    after = nt(x_ref[:, LEFT + raw_len - W:LEFT + raw_len + RIGHT], ft[:, 0:2 * W])
    keep = (t < T - 1) & (lax.broadcasted_iota(jnp.int32, (rows, W), 1) < HALF_WIN)
    put_mag(nb, jnp.where(keep, after, 0.0))

    span = lax.broadcasted_iota(jnp.int32, (2 * W, 4 * W), 1) - W - lax.broadcasted_iota(
        jnp.int32, (2 * W, 4 * W), 0
    )
    band = jnp.where((span >= -HALF_WIN) & (span <= HALF_WIN), 1.0, 0.0).astype(jnp.bfloat16)
    mine = W + t * dec_len

    pr = lax.broadcasted_iota(jnp.int32, (T * SLAB, rows), 0)
    pc = lax.broadcasted_iota(jnp.int32, (T * SLAB, rows), 1)
    picks = jnp.zeros((T * SLAB, rows), jnp.float32)
    for g in range(T):
        for step in range(STEPS):
            for p in range(step_len):
                local = src_ref[step, g * step_len + p] - c * rows
                hit = (pr == g * SLAB + step * step_len + p) & (pc == local)
                picks = jnp.where(hit, 1.0, picks)
    picks = picks.astype(jnp.bfloat16)

    for p in range(nb // 2):
        cols = slice(2 * p * W, (2 * p + 4) * W)
        sums = nt(hi_ref[:, cols], band) + nt(lo_ref[:, cols], band)
        level = sums / (2 * HALF_WIN + 1) + 1e-05
        w = (dec_ref[:, 2 * p * W:2 * (p + 1) * W] / level).astype(jnp.bfloat16)
        white_ref[:, pl.ds(aligned(mine + 2 * p * W), 2 * W)] = w
        rows_of = jnp.dot(picks, w, preferred_element_type=jnp.float32)
        for g in range(T):
            part = rows_of[g * SLAB:(g + 1) * SLAB]
            send1[g * half + p] = jnp.concatenate(
                [part[:, :W], part[:, W:]], axis=0
            ).astype(jnp.bfloat16)

    def first(k, go):
        g, i = k // half, lax.rem(k, half)
        dest = t * half + i
        self_hit = (dest == c) & (g == t)
        remote = pltpu.make_async_remote_copy(
            src_ref=send1.at[k], dst_ref=recv1.at[c],
            send_sem=s1_sem.at[k], recv_sem=r1_sem,
            device_id=(dest, g), device_id_type=MESH,
        )

        @pl.when(jnp.logical_not(self_hit))
        def _():
            if go:
                remote.start()
            else:
                remote.wait_send()

        if go:
            @pl.when(self_hit)
            def _():
                pltpu.make_async_copy(send1.at[k], recv1.at[c], r1_sem).start()

    def each(count, body):
        def step(i, _):
            body(i)
            return 0
        lax.fori_loop(0, count, step, 0)

    each(T * half, lambda k: first(k, True))

    piece = dec_len // PIECES

    def bulk(d, i):
        cols = pl.ds(aligned(mine + i * piece), piece)
        return pltpu.make_async_remote_copy(
            src_ref=white_ref.at[:, cols], dst_ref=white_ref.at[:, cols],
            send_sem=bulk_send.at[d - 1, i], recv_sem=bulk_recv.at[d - 1, i],
            device_id=(c, lax.rem(t + d, T)), device_id_type=MESH,
        )

    for d in range(1, T):
        for i in range(PIECES):
            bulk(d, i).start()

    pltpu.make_async_copy(recv1, recv1, r1_sem).wait()
    summed = recv1[0].astype(jnp.float32)
    for j in range(1, C):
        summed = summed + recv1[j].astype(jnp.float32)
    send1[T * half] = summed.astype(jnp.bfloat16)

    def second(d):
        return pltpu.make_async_remote_copy(
            src_ref=send1.at[T * half], dst_ref=recv2.at[c],
            send_sem=s2_sem.at[d], recv_sem=r2_sem,
            device_id=(lax.rem(c + d + 1, C), t), device_id_type=MESH,
        )

    each(C - 1, lambda d: second(d).start())
    pltpu.make_async_copy(send1.at[T * half], recv2.at[c], r2_sem).start()
    pltpu.make_async_copy(recv2, recv2, r2_sem).wait()

    ahead = lane_id >= row_id
    main = ns * W
    gref[main:main + 16, 0:W] = jnp.zeros((16, W), jnp.bfloat16)
    for s in range(ns):
        def build(j, prev):
            x = recv2[j].astype(jnp.float32)
            for h in range(2):
                now = pltpu.roll(
                    jnp.broadcast_to(x[h * SLAB + s:h * SLAB + s + 1, :], (W, W)),
                    0, 1, stride=1, stride_axis=0,
                )
                gref[s * W:(s + 1) * W, pl.ds(aligned((2 * j + h) * W), W)] = jnp.where(
                    ahead, now, prev
                ).astype(jnp.bfloat16)
                if s == 0:
                    slab = x[h * SLAB:(h + 1) * SLAB]
                    gref[main:main + 16, pl.ds(aligned((2 * j + h + 1) * W), W)] = (
                        jnp.concatenate([slab, slab], axis=0).astype(jnp.bfloat16)
                    )
                prev = now
            return prev

        last = lax.fori_loop(0, C, build, jnp.zeros((W, W), jnp.float32))
        gref[s * W:(s + 1) * W, total:total + W] = jnp.where(ahead, 0.0, last).astype(
            jnp.bfloat16
        )

    def products(a, count):
        both = jnp.concatenate(
            [
                white_ref[:, pl.ds(aligned(a * W), count * W)],
                white_ref[:, pl.ds(aligned(a * W + W), count * W)],
            ],
            axis=0,
        )
        return nt(gref[:, pl.ds(aligned(a * W), count * W)], both)

    acc_ref[...] = products(t * nb + 1, nb - 1)
    step_chunks = nb // PIECES
    for d in range(1, T):
        b = lax.rem(t + T - d, T)
        for i in range(PIECES):
            bulk_in = pltpu.make_async_copy(
                white_ref.at[:, pl.ds(aligned(W + b * dec_len + i * piece), piece)],
                white_ref.at[:, pl.ds(aligned(W + b * dec_len + i * piece), piece)],
                bulk_recv.at[d - 1, i],
            )
            bulk_in.wait()
            skip = 1 if i == 0 else 0
            acc_ref[...] += products(b * nb + i * step_chunks + skip, step_chunks - skip)
    seams = [q * nb * W for q in range(T + 1)]
    both = jnp.concatenate(
        [
            jnp.concatenate([white_ref[:, q:q + W] for q in seams], axis=1),
            jnp.concatenate([white_ref[:, q + W:q + 2 * W] for q in seams], axis=1),
        ],
        axis=0,
    )
    acc_ref[...] += nt(jnp.concatenate([gref[:, q:q + W] for q in seams], axis=1), both)

    for s in range(ns):
        step, p = s // step_len, s % step_len
        out_ref[step, p, 0:W, :] = acc_ref[s * W:(s + 1) * W, 0:W] * scale
        out_ref[step, p, W:2 * W, :] = acc_ref[s * W:(s + 1) * W, W:2 * W] * scale
        out_ref[step, p, 2 * W:2 * W + 1, :] = acc_ref[main + s:main + s + 1, W:2 * W] * scale

    @pl.when(t < T - 1)
    def _():
        to_right.wait_send()

    @pl.when(t > 0)
    def _():
        to_left.wait_send()

    each(T * half, lambda k: first(k, False))
    each(C - 1, lambda d: second(d).wait_send())
    for d in range(1, T):
        for i in range(PIECES):
            bulk(d, i).wait_send()


def per_device(C, T, raw_strain, fir_taps, sources):
    rows, raw_len = raw_strain.shape
    dec_len = raw_len // DECIM
    nb = dec_len // W
    half = nb * C // (T * nb)
    step_len = sources.shape[1] // T
    ns = STEPS * step_len
    total = T * dec_len
    bf, f32 = jnp.bfloat16, jnp.float32
    return pl.pallas_call(
        functools.partial(kernel, C, T, 1.0 / math.sqrt(total)),
        out_shape=jax.ShapeDtypeStruct((STEPS, step_len, LAGS, rows), f32),
        in_specs=[
            pl.BlockSpec(memory_space=pl.ANY),
            pl.BlockSpec(memory_space=pltpu.VMEM),
            pl.BlockSpec(memory_space=pltpu.SMEM),
        ],
        out_specs=pl.BlockSpec(memory_space=pltpu.VMEM),
        scratch_shapes=[
            pltpu.VMEM((rows, LEFT + raw_len + RIGHT), bf),
            pltpu.VMEM((rows, dec_len), f32),
            pltpu.VMEM((rows, dec_len + 2 * W), bf),
            pltpu.VMEM((rows, dec_len + 2 * W), bf),
            pltpu.VMEM((rows, total + 2 * W), bf),
            pltpu.VMEM((T * half + 1, 16, W), bf),
            pltpu.VMEM((C, 16, W), bf),
            pltpu.VMEM((C, 16, W), bf),
            pltpu.VMEM((ns * W + 16, total + W), bf),
            pltpu.VMEM((ns * W + 16, 2 * W), f32),
            pltpu.SemaphoreType.DMA((PIECES,)),
            pltpu.SemaphoreType.DMA((2,)),
            pltpu.SemaphoreType.DMA((2,)),
            pltpu.SemaphoreType.DMA((T * half,)),
            pltpu.SemaphoreType.DMA,
            pltpu.SemaphoreType.DMA((C,)),
            pltpu.SemaphoreType.DMA,
            pltpu.SemaphoreType.DMA,
            pltpu.SemaphoreType.DMA((T, PIECES)),
            pltpu.SemaphoreType.DMA((T, PIECES)),
        ],
        compiler_params=pltpu.CompilerParams(
            collective_id=0, has_side_effects=True, vmem_limit_bytes=40 * 1024 * 1024
        ),
    )(raw_strain, fir_taps.reshape(1, TAPS), sources)


def solution(mesh):
    C, T = mesh.shape["chan"], mesh.shape["tm"]
    return jax.shard_map(
        functools.partial(per_device, C, T),
        mesh=mesh,
        in_specs=(P("chan", "tm"), P(), P()),
        out_specs=P(None, "tm", None, "chan"),
        check_vma=False,
    )
```

```python
import functools
import math

import jax
import jax.numpy as jnp
from jax import lax
from jax.experimental import pallas as pl
from jax.experimental.pallas import tpu as pltpu
from jax.sharding import PartitionSpec as P

TAPS = 64
DECIM = 4
HALF_WIN = 32
LAGS = 257
HALF_LAG = 128
STEPS = 2
W = 128
SLAB = 8
PIECES = 4
LEFT = 256
RIGHT = 128
MESH = pl.DeviceIdType.MESH


def nt(a, b):
    return lax.dot_general(
        a, b, (((1,), (1,)), ((), ())), preferred_element_type=jnp.float32
    )


def aligned(x):
    return pl.multiple_of(x, W)


def kernel(
    C, T, scale,
    raw_ref, taps_hbm, src_hbm, out_ref,
    taps_ref, src_ref, praw_ref, rep_ref, x_ref, dec_ref, hi_ref, lo_ref, white_ref, send1, recv1, recv2, gref, acc_ref,
    small_sem, load_sem, halo_send, halo_recv, s1_sem, r1_sem, s2_sem, r2_sem, own_sem, bulk_send, bulk_recv,
):
    c = lax.axis_index("chan")
    t = lax.axis_index("tm")
    N = C * T
    rows, raw_len = raw_ref.shape
    dec_len = raw_len // DECIM
    nb = dec_len // W
    per_dev = (T * nb) // C
    half = nb // per_dev
    step_len = src_hbm.shape[1] // T
    ns = STEPS * step_len
    me = c * T + t

    barrier = pltpu.get_barrier_semaphore()

    def greet(d, _):
        other = lax.rem(me + d, N)
        pl.semaphore_signal(
            barrier, inc=1, device_id=(other // T, lax.rem(other, T)), device_id_type=MESH
        )
        return 0

    lax.fori_loop(1, N, greet, 0)

    small = [
        pltpu.make_async_copy(taps_hbm, taps_ref, small_sem.at[0]),
        pltpu.make_async_copy(src_hbm, src_ref, small_sem.at[1]),
    ]
    for copy in small:
        copy.start()
    seg = raw_len // PIECES
    loads = []
    for i in range(PIECES):
        load = pltpu.make_async_copy(
            raw_ref.at[:, pl.ds(i * seg, seg)],
            x_ref.at[:, pl.ds(LEFT + i * seg, seg)],
            load_sem.at[i],
        )
        load.start()
        loads.append(load)

    for copy in small:
        copy.wait()

    taps = jnp.broadcast_to(taps_ref[...], (16, TAPS))
    place = lax.broadcasted_iota(jnp.int32, (TAPS, W), 1) == lax.rem(
        W - lax.broadcasted_iota(jnp.int32, (TAPS, W), 0), W
    )
    base = jnp.dot(
        taps, place.astype(jnp.float32).astype(jnp.bfloat16), preferred_element_type=jnp.float32
    )
    rolled = pltpu.roll(
        jnp.broadcast_to(base[0:1, :], (W, W)), 0, 1, stride=DECIM, stride_axis=0
    )
    row_id = lax.broadcasted_iota(jnp.int32, (W, W), 0)
    lane_id = lax.broadcasted_iota(jnp.int32, (W, W), 1)
    fts = []
    for jc in range(DECIM + 1):
        k = DECIM * row_id + W - W * jc - lane_id
        fts.append(jnp.where((k >= 0) & (k < W), rolled, 0.0).astype(jnp.bfloat16))
    ft = jnp.concatenate(fts, axis=1)

    pr = lax.broadcasted_iota(jnp.int32, (T * SLAB, rows), 0)
    pc = lax.broadcasted_iota(jnp.int32, (T * SLAB, rows), 1)
    picks = jnp.zeros((T * SLAB, rows), jnp.float32)
    for g in range(T):
        for step in range(STEPS):
            for p in range(step_len):
                local = src_ref[step, g * step_len + p] - c * rows
                hit = (pr == g * SLAB + step * step_len + p) & (pc == local)
                picks = jnp.where(hit, 1.0, picks)
    picks = picks.astype(jnp.bfloat16)

    pl.semaphore_wait(barrier, N - 1)

    to_right = pltpu.make_async_remote_copy(
        src_ref=raw_ref.at[:, pl.ds(raw_len - LEFT, LEFT)],
        dst_ref=x_ref.at[:, pl.ds(0, LEFT)],
        send_sem=halo_send.at[0], recv_sem=halo_recv.at[0],
        device_id=(c, lax.rem(t + 1, T)), device_id_type=MESH,
    )
    to_left = pltpu.make_async_remote_copy(
        src_ref=raw_ref.at[:, pl.ds(0, RIGHT)],
        dst_ref=x_ref.at[:, pl.ds(LEFT + raw_len, RIGHT)],
        send_sem=halo_send.at[1], recv_sem=halo_recv.at[1],
        device_id=(c, lax.rem(t + T - 1, T)), device_id_type=MESH,
    )

    @pl.when(t < T - 1)
    def _():
        to_right.start()

    @pl.when(t > 0)
    def _():
        to_left.start()

    @pl.when(t == 0)
    def _():
        x_ref[:, 0:LEFT] = jnp.zeros((rows, LEFT), jnp.bfloat16)

    @pl.when(t == T - 1)
    def _():
        x_ref[:, LEFT + raw_len:] = jnp.zeros((rows, RIGHT), jnp.bfloat16)

    total = T * dec_len
    white_ref[:, 0:W] = jnp.zeros((rows, W), jnp.bfloat16)
    white_ref[:, W + total:] = jnp.zeros((rows, W), jnp.bfloat16)

    def put_mag(b, d):
        mag = jnp.abs(d)
        hi = mag.astype(jnp.bfloat16)
        hi_ref[:, (b + 1) * W:(b + 2) * W] = hi
        lo_ref[:, (b + 1) * W:(b + 2) * W] = (mag - hi.astype(jnp.float32)).astype(jnp.bfloat16)

    def chunk(b):
        begin = LEFT - W + b * DECIM * W
        d = nt(x_ref[:, begin:begin + (DECIM + 1) * W], ft)
        dec_ref[:, b * W:(b + 1) * W] = d
        put_mag(b, d)

    def pick_raw(x):
        return jnp.dot(picks, x, preferred_element_type=jnp.float32).astype(jnp.bfloat16)

    lead = (DECIM + 1) * W
    many = T * SLAB
    praw_ref[:, 0:lead - LEFT] = jnp.zeros((many, lead - LEFT), jnp.bfloat16)
    praw_ref[:, lead + raw_len + RIGHT:] = jnp.zeros((many, DECIM * W - RIGHT), jnp.bfloat16)
    for i in range(PIECES):
        loads[i].wait()
        praw_ref[:, lead + i * seg:lead + (i + 1) * seg] = pick_raw(
            x_ref[:, LEFT + i * seg:LEFT + (i + 1) * seg]
        )
    for b in range(1, nb):
        chunk(b)

    @pl.when(t > 0)
    def _():
        to_right.wait_recv()

    @pl.when(t < T - 1)
    def _():
        to_left.wait_recv()

    praw_ref[:, lead - LEFT:lead] = pick_raw(x_ref[:, 0:LEFT])
    praw_ref[:, lead + raw_len:lead + raw_len + RIGHT] = pick_raw(x_ref[:, LEFT + raw_len:])
    picked = nt(
        jnp.concatenate(
            [praw_ref[:, b * DECIM * W:b * DECIM * W + lead] for b in range(nb + 2)], axis=0
        ),
        ft,
    )
    size = (nb + 2) * many
    pr = lax.broadcasted_iota(jnp.int32, (size, W), 0)
    pc = lax.broadcasted_iota(jnp.int32, (size, W), 1)
    inside = ((pr >= many) | ((t > 0) & (pc >= W - HALF_WIN))) & (
        (pr < size - many) | ((t < T - 1) & (pc < HALF_WIN))
    )
    mag = jnp.where(inside, jnp.abs(picked), 0.0)
    hi = mag.astype(jnp.bfloat16)
    lo = (mag - hi.astype(jnp.float32)).astype(jnp.bfloat16)
    wide = jnp.concatenate(
        [m[k * many:k * many + nb * many] for m in (hi, lo) for k in range(3)], axis=1
    )
    span = lax.broadcasted_iota(jnp.int32, (W, 3 * W), 1) - W - lax.broadcasted_iota(
        jnp.int32, (W, 3 * W), 0
    )
    band = jnp.where((span >= -HALF_WIN) & (span <= HALF_WIN), 1.0, 0.0).astype(jnp.bfloat16)
    level = nt(wide, jnp.concatenate([band, band], axis=1)) / (2 * HALF_WIN + 1) + 1e-05
    picked = picked[many:many + nb * many] / level
    for g in range(T):
        for i in range(half):
            send1[g * half + i] = jnp.concatenate(
                [
                    picked[q * many + g * SLAB:q * many + (g + 1) * SLAB]
                    for q in (2 * i, 2 * i + 1)
                ],
                axis=0,
            ).astype(jnp.bfloat16)

    def first(k, go):
        g, i = k // half, k % half
        dest = t * half + i
        self_hit = (dest == c) & (g == t)
        remote = pltpu.make_async_remote_copy(
            src_ref=send1.at[k], dst_ref=recv1.at[c],
            send_sem=s1_sem.at[k], recv_sem=r1_sem,
            device_id=(dest, g), device_id_type=MESH,
        )

        @pl.when(jnp.logical_not(self_hit))
        def _():
            if go:
                remote.start()
            else:
                remote.wait_send()

        if go:
            @pl.when(self_hit)
            def _():
                pltpu.make_async_copy(send1.at[k], recv1.at[c], r1_sem).start()

    def each(count, body):
        if count <= 16:
            for i in range(count):
                body(i)
            return

        def step(i, _):
            body(i)
            return 0

        lax.fori_loop(0, count, step, 0)

    each(T * half, lambda k: first(k, True))

    chunk(0)
    before = nt(x_ref[:, 0:LEFT], ft[:, 3 * W:5 * W])
    keep = (t > 0) & (lax.broadcasted_iota(jnp.int32, (rows, W), 1) >= W - HALF_WIN)
    put_mag(-1, jnp.where(keep, before, 0.0))
    after = nt(x_ref[:, LEFT + raw_len - W:LEFT + raw_len + RIGHT], ft[:, 0:2 * W])
    keep = (t < T - 1) & (lax.broadcasted_iota(jnp.int32, (rows, W), 1) < HALF_WIN)
    put_mag(nb, jnp.where(keep, after, 0.0))

    span = lax.broadcasted_iota(jnp.int32, (2 * W, 4 * W), 1) - W - lax.broadcasted_iota(
        jnp.int32, (2 * W, 4 * W), 0
    )
    band = jnp.where((span >= -HALF_WIN) & (span <= HALF_WIN), 1.0, 0.0).astype(jnp.bfloat16)
    mine = W + t * dec_len

    piece = dec_len // PIECES

    def bulk(d, i):
        cols = pl.ds(aligned(mine + i * piece), piece)
        return pltpu.make_async_remote_copy(
            src_ref=white_ref.at[:, cols], dst_ref=white_ref.at[:, cols],
            send_sem=bulk_send.at[d - 1, i], recv_sem=bulk_recv.at[d - 1, i],
            device_id=(c, lax.rem(t + d, T)), device_id_type=MESH,
        )

    for p in range(nb // 2):
        cols = slice(2 * p * W, (2 * p + 4) * W)
        sums = nt(hi_ref[:, cols], band) + nt(lo_ref[:, cols], band)
        level = sums / (2 * HALF_WIN + 1) + 1e-05
        w = (dec_ref[:, 2 * p * W:2 * (p + 1) * W] / level).astype(jnp.bfloat16)
        white_ref[:, pl.ds(aligned(mine + 2 * p * W), 2 * W)] = w
        if (2 * p + 2) * W % piece == 0:
            for d in range(1, T):
                bulk(d, (2 * p + 2) * W // piece - 1).start()

    pltpu.make_async_copy(recv1, recv1, r1_sem).wait()
    summed = recv1[0].astype(jnp.float32)
    for j in range(1, C):
        summed = summed + recv1[j].astype(jnp.float32)
    send1[T * half] = summed.astype(jnp.bfloat16)

    def second(d):
        return pltpu.make_async_remote_copy(
            src_ref=send1.at[T * half], dst_ref=recv2.at[c],
            send_sem=s2_sem.at[d], recv_sem=r2_sem,
            device_id=(lax.rem(c + d + 1, C), t), device_id_type=MESH,
        )

    each(C - 1, lambda d: second(d).start())
    pltpu.make_async_copy(send1.at[T * half], recv2.at[c], r2_sem).start()
    pltpu.make_async_copy(recv2, recv2, r2_sem).wait()

    group = 16 // step_len
    main = ns * W
    gathered = jnp.concatenate([recv2[j] for j in range(C)], axis=1)
    spread_row = lax.broadcasted_iota(jnp.int32, (2 * STEPS * 16, 16), 0)
    spread_col = lax.broadcasted_iota(jnp.int32, (2 * STEPS * 16, 16), 1)
    wanted = (spread_row // (STEPS * 16)) * SLAB + (spread_row // 16 % STEPS) * step_len + (
        spread_row % step_len
    )
    spread = jnp.where(spread_col == wanted, 1.0, 0.0).astype(jnp.bfloat16)
    rep_ref[...] = jnp.dot(spread, gathered, preferred_element_type=jnp.float32).astype(
        jnp.bfloat16
    )
    slabs = gathered.astype(jnp.float32)
    gref[main:main + 16, 0:W] = jnp.zeros((16, W), jnp.bfloat16)
    for q in range(2 * C):
        slab = slabs[q % 2 * SLAB:(q % 2 + 1) * SLAB, q // 2 * W:(q // 2 + 1) * W]
        gref[main:main + 16, (q + 1) * W:(q + 2) * W] = jnp.concatenate(
            [slab, slab], axis=0
        ).astype(jnp.bfloat16)
    low = (lax.broadcasted_iota(jnp.int32, (16, W), 0) // step_len)
    low_lane = (lax.broadcasted_iota(jnp.int32, (16, W), 1) - low).astype(jnp.int16)
    low = low.astype(jnp.int16)
    tiles = W // group
    for step in range(STEPS):
        first_row = step * step_len * W

        def tile(a, now, prev, column):
            gref[first_row + a * 16:first_row + (a + 1) * 16, pl.ds(column, W)] = jnp.where(
                low_lane >= a * group, now, prev
            )

        def build(j, prev):
            for h in range(2):
                top = (h * STEPS + step) * 16
                x = rep_ref[top:top + 16, pl.ds(aligned(j * W), W)]
                start = x
                for k in range(1, group):
                    start = jnp.where(low == k, pltpu.roll(x, k, 1), start)
                out = []
                for a in range(tiles):
                    now = pltpu.roll(start, a * group, 1) if a else start
                    tile(a, now, prev[a], aligned((2 * j + h) * W))
                    out.append(now)
                prev = tuple(out)
            return prev

        last = lax.fori_loop(0, C, build, (jnp.zeros((16, W), jnp.bfloat16),) * tiles)
        for a in range(tiles):
            tile(a, jnp.zeros((16, W), jnp.bfloat16), last[a], total)

    def products(a, count):
        both = jnp.concatenate(
            [
                white_ref[:, pl.ds(aligned(a * W), count * W)],
                white_ref[:, pl.ds(aligned(a * W + W), count * W)],
            ],
            axis=0,
        )
        return nt(gref[:, pl.ds(aligned(a * W), count * W)], both)

    acc_ref[...] = products(t * nb + 1, nb - 1)
    step_chunks = nb // PIECES
    for d in range(1, T):
        b = lax.rem(t + T - d, T)
        for i in range(PIECES):
            bulk_in = pltpu.make_async_copy(
                white_ref.at[:, pl.ds(aligned(W + b * dec_len + i * piece), piece)],
                white_ref.at[:, pl.ds(aligned(W + b * dec_len + i * piece), piece)],
                bulk_recv.at[d - 1, i],
            )
            bulk_in.wait()
            skip = 1 if i == 0 else 0
            acc_ref[...] += products(b * nb + i * step_chunks + skip, step_chunks - skip)
    seams = [q * nb * W for q in range(T + 1)]
    both = jnp.concatenate(
        [
            jnp.concatenate([white_ref[:, q:q + W] for q in seams], axis=1),
            jnp.concatenate([white_ref[:, q + W:q + 2 * W] for q in seams], axis=1),
        ],
        axis=0,
    )
    acc_ref[...] += nt(jnp.concatenate([gref[:, q:q + W] for q in seams], axis=1), both)

    span = step_len * W
    for step in range(STEPS):
        at, to = step * span, step * step_len * LAGS
        out_ref[to:to + span, :] = acc_ref[at:at + span, 0:W] * scale
        out_ref[to + span:to + 2 * span, :] = acc_ref[at:at + span, W:2 * W] * scale
        extra = main + step * step_len
        out_ref[to + 2 * span:to + 2 * span + step_len, :] = (
            acc_ref[extra:extra + step_len, W:2 * W] * scale
        )

    @pl.when(t < T - 1)
    def _():
        to_right.wait_send()

    @pl.when(t > 0)
    def _():
        to_left.wait_send()

    each(T * half, lambda k: first(k, False))
    each(C - 1, lambda d: second(d).wait_send())
    for d in range(1, T):
        for i in range(PIECES):
            bulk(d, i).wait_send()


def per_device(C, T, raw_strain, fir_taps, sources):
    rows, raw_len = raw_strain.shape
    dec_len = raw_len // DECIM
    nb = dec_len // W
    half = nb * C // (T * nb)
    step_len = sources.shape[1] // T
    ns = STEPS * step_len
    total = T * dec_len
    bf, f32 = jnp.bfloat16, jnp.float32
    flat = pl.pallas_call(
        functools.partial(kernel, C, T, 1.0 / math.sqrt(total)),
        out_shape=jax.ShapeDtypeStruct((STEPS * LAGS * step_len, rows), f32),
        in_specs=[
            pl.BlockSpec(memory_space=pltpu.HBM),
            pl.BlockSpec(memory_space=pltpu.HBM),
            pl.BlockSpec(memory_space=pltpu.HBM),
        ],
        out_specs=pl.BlockSpec(memory_space=pltpu.VMEM),
        scratch_shapes=[
            pltpu.VMEM((1, TAPS), bf),
            pltpu.SMEM(sources.shape, jnp.int32),
            pltpu.VMEM((T * SLAB, raw_len + (2 * DECIM + 1) * W), bf),
            pltpu.VMEM((2 * STEPS * 16, C * W), bf),
            pltpu.VMEM((rows, LEFT + raw_len + RIGHT), bf),
            pltpu.VMEM((rows, dec_len), f32),
            pltpu.VMEM((rows, dec_len + 2 * W), bf),
            pltpu.VMEM((rows, dec_len + 2 * W), bf),
            pltpu.VMEM((rows, total + 2 * W), bf),
            pltpu.VMEM((T * half + 1, 16, W), bf),
            pltpu.VMEM((C, 16, W), bf),
            pltpu.VMEM((C, 16, W), bf),
            pltpu.VMEM((ns * W + 16, total + W), bf),
            pltpu.VMEM((ns * W + 16, 2 * W), f32),
            pltpu.SemaphoreType.DMA((2,)),
            pltpu.SemaphoreType.DMA((PIECES,)),
            pltpu.SemaphoreType.DMA((2,)),
            pltpu.SemaphoreType.DMA((2,)),
            pltpu.SemaphoreType.DMA((T * half,)),
            pltpu.SemaphoreType.DMA,
            pltpu.SemaphoreType.DMA((C,)),
            pltpu.SemaphoreType.DMA,
            pltpu.SemaphoreType.DMA,
            pltpu.SemaphoreType.DMA((T, PIECES)),
            pltpu.SemaphoreType.DMA((T, PIECES)),
        ],
        compiler_params=pltpu.CompilerParams(
            collective_id=0, has_side_effects=True, vmem_limit_bytes=62 * 1024 * 1024
        ),
    )(raw_strain, fir_taps.reshape(1, TAPS), sources)
    return jnp.swapaxes(flat.reshape(STEPS, LAGS, step_len, rows), 1, 2)


def solution(mesh):
    C, T = mesh.shape["chan"], mesh.shape["tm"]
    return jax.shard_map(
        functools.partial(per_device, C, T),
        mesh=mesh,
        in_specs=(P("chan", "tm"), P(), P()),
        out_specs=P(None, "tm", None, "chan"),
        check_vma=False,
    )
```

```python
import functools
import math

import jax
import jax.numpy as jnp
from jax import lax
from jax.experimental import pallas as pl
from jax.experimental.pallas import tpu as pltpu
from jax.sharding import PartitionSpec as P

TAPS = 64
DECIM = 4
HALF_WIN = 32
LAGS = 257
HALF_LAG = 128
STEPS = 2
W = 128
SLAB = 8
PIECES = 4
LEFT = 256
RIGHT = 128
MESH = pl.DeviceIdType.MESH


def nt(a, b):
    return lax.dot_general(
        a, b, (((1,), (1,)), ((), ())), preferred_element_type=jnp.float32
    )


def aligned(x):
    return pl.multiple_of(x, W)


def kernel(
    C, T, scale,
    raw_ref, taps_hbm, src_hbm, out_ref,
    taps_ref, src_ref, praw_ref, rep_ref, x_ref, dec_ref, hi_ref, lo_ref, white_ref, send1, recv1, recv2, gref, acc_ref,
    small_sem, load_sem, halo_send, halo_recv, s1_sem, r1_sem, s2_sem, r2_sem, own_sem, bulk_send, bulk_recv,
):
    c = lax.axis_index("chan")
    t = lax.axis_index("tm")
    N = C * T
    rows, raw_len = raw_ref.shape
    dec_len = raw_len // DECIM
    nb = dec_len // W
    per_dev = (T * nb) // C
    half = nb // per_dev
    step_len = src_hbm.shape[1] // T
    ns = STEPS * step_len
    me = c * T + t

    barrier = pltpu.get_barrier_semaphore()

    def greet(d, _):
        other = lax.rem(me + d, N)
        pl.semaphore_signal(
            barrier, inc=1, device_id=(other // T, lax.rem(other, T)), device_id_type=MESH
        )
        return 0

    lax.fori_loop(1, N, greet, 0)

    small = [
        pltpu.make_async_copy(taps_hbm, taps_ref, small_sem.at[0]),
        pltpu.make_async_copy(src_hbm, src_ref, small_sem.at[1]),
    ]
    for copy in small:
        copy.start()
    seg = raw_len // PIECES
    loads = []
    for i in range(PIECES):
        load = pltpu.make_async_copy(
            raw_ref.at[:, pl.ds(i * seg, seg)],
            x_ref.at[:, pl.ds(LEFT + i * seg, seg)],
            load_sem.at[i],
        )
        load.start()
        loads.append(load)

    for copy in small:
        copy.wait()

    taps = jnp.broadcast_to(taps_ref[...], (16, TAPS))
    place = lax.broadcasted_iota(jnp.int32, (TAPS, W), 1) == lax.rem(
        W - lax.broadcasted_iota(jnp.int32, (TAPS, W), 0), W
    )
    base = jnp.dot(
        taps, place.astype(jnp.float32).astype(jnp.bfloat16), preferred_element_type=jnp.float32
    )
    rolled = pltpu.roll(
        jnp.broadcast_to(base[0:1, :], (W, W)), 0, 1, stride=DECIM, stride_axis=0
    )
    row_id = lax.broadcasted_iota(jnp.int32, (W, W), 0)
    lane_id = lax.broadcasted_iota(jnp.int32, (W, W), 1)
    fts = []
    for jc in range(DECIM + 1):
        k = DECIM * row_id + W - W * jc - lane_id
        fts.append(jnp.where((k >= 0) & (k < W), rolled, 0.0).astype(jnp.bfloat16))
    ft = jnp.concatenate(fts, axis=1)

    pr = lax.broadcasted_iota(jnp.int32, (T * SLAB, rows), 0)
    pc = lax.broadcasted_iota(jnp.int32, (T * SLAB, rows), 1)
    picks = jnp.zeros((T * SLAB, rows), jnp.float32)
    for g in range(T):
        for step in range(STEPS):
            for p in range(step_len):
                local = src_ref[step, g * step_len + p] - c * rows
                hit = (pr == g * SLAB + step * step_len + p) & (pc == local)
                picks = jnp.where(hit, 1.0, picks)
    picks = picks.astype(jnp.bfloat16)

    pl.semaphore_wait(barrier, N - 1)

    to_right = pltpu.make_async_remote_copy(
        src_ref=raw_ref.at[:, pl.ds(raw_len - LEFT, LEFT)],
        dst_ref=x_ref.at[:, pl.ds(0, LEFT)],
        send_sem=halo_send.at[0], recv_sem=halo_recv.at[0],
        device_id=(c, lax.rem(t + 1, T)), device_id_type=MESH,
    )
    to_left = pltpu.make_async_remote_copy(
        src_ref=raw_ref.at[:, pl.ds(0, RIGHT)],
        dst_ref=x_ref.at[:, pl.ds(LEFT + raw_len, RIGHT)],
        send_sem=halo_send.at[1], recv_sem=halo_recv.at[1],
        device_id=(c, lax.rem(t + T - 1, T)), device_id_type=MESH,
    )

    @pl.when(t < T - 1)
    def _():
        to_right.start()

    @pl.when(t > 0)
    def _():
        to_left.start()

    @pl.when(t == 0)
    def _():
        x_ref[:, 0:LEFT] = jnp.zeros((rows, LEFT), jnp.bfloat16)

    @pl.when(t == T - 1)
    def _():
        x_ref[:, LEFT + raw_len:] = jnp.zeros((rows, RIGHT), jnp.bfloat16)

    total = T * dec_len
    white_ref[:, 0:W] = jnp.zeros((rows, W), jnp.bfloat16)
    white_ref[:, W + total:] = jnp.zeros((rows, W), jnp.bfloat16)

    def put_mag(b, d):
        mag = jnp.abs(d)
        hi = mag.astype(jnp.bfloat16)
        hi_ref[:, (b + 1) * W:(b + 2) * W] = hi
        lo_ref[:, (b + 1) * W:(b + 2) * W] = (mag - hi.astype(jnp.float32)).astype(jnp.bfloat16)

    def chunk(b):
        begin = LEFT - W + b * DECIM * W
        d = nt(x_ref[:, begin:begin + (DECIM + 1) * W], ft)
        dec_ref[:, b * W:(b + 1) * W] = d
        put_mag(b, d)

    def pick_raw(x):
        return jnp.dot(picks, x, preferred_element_type=jnp.float32).astype(jnp.bfloat16)

    lead = (DECIM + 1) * W
    many = T * SLAB
    praw_ref[:, 0:lead - LEFT] = jnp.zeros((many, lead - LEFT), jnp.bfloat16)
    praw_ref[:, lead + raw_len + RIGHT:] = jnp.zeros((many, DECIM * W - RIGHT), jnp.bfloat16)
    for i in range(PIECES):
        loads[i].wait()
        praw_ref[:, lead + i * seg:lead + (i + 1) * seg] = pick_raw(
            x_ref[:, LEFT + i * seg:LEFT + (i + 1) * seg]
        )
    for b in range(1, nb):
        chunk(b)

    @pl.when(t > 0)
    def _():
        to_right.wait_recv()

    @pl.when(t < T - 1)
    def _():
        to_left.wait_recv()

    praw_ref[:, lead - LEFT:lead] = pick_raw(x_ref[:, 0:LEFT])
    praw_ref[:, lead + raw_len:lead + raw_len + RIGHT] = pick_raw(x_ref[:, LEFT + raw_len:])
    picked = nt(
        jnp.concatenate(
            [praw_ref[:, b * DECIM * W:b * DECIM * W + lead] for b in range(nb + 2)], axis=0
        ),
        ft,
    )
    size = (nb + 2) * many
    pr = lax.broadcasted_iota(jnp.int32, (size, W), 0)
    pc = lax.broadcasted_iota(jnp.int32, (size, W), 1)
    inside = ((pr >= many) | ((t > 0) & (pc >= W - HALF_WIN))) & (
        (pr < size - many) | ((t < T - 1) & (pc < HALF_WIN))
    )
    mag = jnp.where(inside, jnp.abs(picked), 0.0)
    hi = mag.astype(jnp.bfloat16)
    lo = (mag - hi.astype(jnp.float32)).astype(jnp.bfloat16)
    wide = jnp.concatenate(
        [m[k * many:k * many + nb * many] for m in (hi, lo) for k in range(3)], axis=1
    )
    span = lax.broadcasted_iota(jnp.int32, (W, 3 * W), 1) - W - lax.broadcasted_iota(
        jnp.int32, (W, 3 * W), 0
    )
    band = jnp.where((span >= -HALF_WIN) & (span <= HALF_WIN), 1.0, 0.0).astype(jnp.bfloat16)
    level = nt(wide, jnp.concatenate([band, band], axis=1)) / (2 * HALF_WIN + 1) + 1e-05
    picked = picked[many:many + nb * many] / level
    for g in range(T):
        for i in range(half):
            send1[g * half + i] = jnp.concatenate(
                [
                    picked[q * many + g * SLAB:q * many + (g + 1) * SLAB]
                    for q in (2 * i, 2 * i + 1)
                ],
                axis=0,
            ).astype(jnp.bfloat16)

    def first(k, go):
        g, i = k // half, k % half
        dest = t * half + i
        self_hit = (dest == c) & (g == t)
        remote = pltpu.make_async_remote_copy(
            src_ref=send1.at[k], dst_ref=recv1.at[c],
            send_sem=s1_sem.at[k], recv_sem=r1_sem,
            device_id=(dest, g), device_id_type=MESH,
        )

        @pl.when(jnp.logical_not(self_hit))
        def _():
            if go:
                remote.start()
            else:
                remote.wait_send()

        if go:
            @pl.when(self_hit)
            def _():
                pltpu.make_async_copy(send1.at[k], recv1.at[c], r1_sem).start()

    def each(count, body):
        if count <= 16:
            for i in range(count):
                body(i)
            return

        def step(i, _):
            body(i)
            return 0

        lax.fori_loop(0, count, step, 0)

    each(T * half, lambda k: first(k, True))

    chunk(0)
    before = nt(x_ref[:, 0:LEFT], ft[:, 3 * W:5 * W])
    keep = (t > 0) & (lax.broadcasted_iota(jnp.int32, (rows, W), 1) >= W - HALF_WIN)
    put_mag(-1, jnp.where(keep, before, 0.0))
    after = nt(x_ref[:, LEFT + raw_len - W:LEFT + raw_len + RIGHT], ft[:, 0:2 * W])
    keep = (t < T - 1) & (lax.broadcasted_iota(jnp.int32, (rows, W), 1) < HALF_WIN)
    put_mag(nb, jnp.where(keep, after, 0.0))

    span = lax.broadcasted_iota(jnp.int32, (2 * W, 4 * W), 1) - W - lax.broadcasted_iota(
        jnp.int32, (2 * W, 4 * W), 0
    )
    band = jnp.where((span >= -HALF_WIN) & (span <= HALF_WIN), 1.0, 0.0).astype(jnp.bfloat16)
    mine = W + t * dec_len

    piece = dec_len // PIECES

    def bulk(d, i):
        cols = pl.ds(aligned(mine + i * piece), piece)
        return pltpu.make_async_remote_copy(
            src_ref=white_ref.at[:, cols], dst_ref=white_ref.at[:, cols],
            send_sem=bulk_send.at[d - 1, i], recv_sem=bulk_recv.at[d - 1, i],
            device_id=(c, lax.rem(t + d, T)), device_id_type=MESH,
        )

    for p in range(nb // 2):
        cols = slice(2 * p * W, (2 * p + 4) * W)
        sums = nt(hi_ref[:, cols], band) + nt(lo_ref[:, cols], band)
        level = sums / (2 * HALF_WIN + 1) + 1e-05
        w = (dec_ref[:, 2 * p * W:2 * (p + 1) * W] / level).astype(jnp.bfloat16)
        white_ref[:, pl.ds(aligned(mine + 2 * p * W), 2 * W)] = w
        if (2 * p + 2) * W % piece == 0:
            for d in range(1, T):
                bulk(d, (2 * p + 2) * W // piece - 1).start()

    pltpu.make_async_copy(recv1, recv1, r1_sem).wait()
    summed = recv1[0].astype(jnp.float32)
    for j in range(1, C):
        summed = summed + recv1[j].astype(jnp.float32)
    send1[T * half] = summed.astype(jnp.bfloat16)

    def second(d):
        return pltpu.make_async_remote_copy(
            src_ref=send1.at[T * half], dst_ref=recv2.at[c],
            send_sem=s2_sem.at[d], recv_sem=r2_sem,
            device_id=(lax.rem(c + d + 1, C), t), device_id_type=MESH,
        )

    each(C - 1, lambda d: second(d).start())
    pltpu.make_async_copy(send1.at[T * half], recv2.at[c], r2_sem).start()
    pltpu.make_async_copy(recv2, recv2, r2_sem).wait()

    group = 16 // step_len
    main = ns * W
    gathered = jnp.concatenate([recv2[j] for j in range(C)], axis=1)
    spread_row = lax.broadcasted_iota(jnp.int32, (2 * STEPS * 16, 16), 0)
    spread_col = lax.broadcasted_iota(jnp.int32, (2 * STEPS * 16, 16), 1)
    wanted = (spread_row // (STEPS * 16)) * SLAB + (spread_row // 16 % STEPS) * step_len + (
        spread_row % step_len
    )
    spread = jnp.where(spread_col == wanted, 1.0, 0.0).astype(jnp.bfloat16)
    rep_ref[...] = jnp.dot(spread, gathered, preferred_element_type=jnp.float32).astype(
        jnp.bfloat16
    )
    slabs = gathered.astype(jnp.float32)
    gref[main:main + 16, 0:W] = jnp.zeros((16, W), jnp.bfloat16)
    for q in range(2 * C):
        slab = slabs[q % 2 * SLAB:(q % 2 + 1) * SLAB, q // 2 * W:(q // 2 + 1) * W]
        gref[main:main + 16, (q + 1) * W:(q + 2) * W] = jnp.concatenate(
            [slab, slab], axis=0
        ).astype(jnp.bfloat16)
    low = (lax.broadcasted_iota(jnp.int32, (16, W), 0) // step_len)
    low_lane = (lax.broadcasted_iota(jnp.int32, (16, W), 1) - low).astype(jnp.int16)
    low = low.astype(jnp.int16)
    tiles = W // group
    for step in range(STEPS):
        first_row = step * step_len * W

        def tile(a, now, prev, column):
            gref[first_row + a * 16:first_row + (a + 1) * 16, pl.ds(column, W)] = jnp.where(
                low_lane >= a * group, now, prev
            )

        def build(j, prev):
            for h in range(2):
                top = (h * STEPS + step) * 16
                x = rep_ref[top:top + 16, pl.ds(aligned(j * W), W)]
                start = x
                for k in range(1, group):
                    start = jnp.where(low == k, pltpu.roll(x, k, 1), start)
                out = []
                for a in range(tiles):
                    now = pltpu.roll(start, a * group, 1) if a else start
                    tile(a, now, prev[a], aligned((2 * j + h) * W))
                    out.append(now)
                prev = tuple(out)
            return prev

        last = lax.fori_loop(0, C, build, (jnp.zeros((16, W), jnp.bfloat16),) * tiles)
        for a in range(tiles):
            tile(a, jnp.zeros((16, W), jnp.bfloat16), last[a], total)

    def products(a, count):
        both = jnp.concatenate(
            [
                white_ref[:, pl.ds(aligned(a * W), count * W)],
                white_ref[:, pl.ds(aligned(a * W + W), count * W)],
            ],
            axis=0,
        )
        return nt(gref[:, pl.ds(aligned(a * W), count * W)], both)

    acc_ref[...] = products(t * nb + 1, nb - 1)
    step_chunks = nb // PIECES
    for d in range(1, T):
        b = lax.rem(t + T - d, T)
        for i in range(PIECES):
            bulk_in = pltpu.make_async_copy(
                white_ref.at[:, pl.ds(aligned(W + b * dec_len + i * piece), piece)],
                white_ref.at[:, pl.ds(aligned(W + b * dec_len + i * piece), piece)],
                bulk_recv.at[d - 1, i],
            )
            bulk_in.wait()
            skip = 1 if i == 0 else 0
            acc_ref[...] += products(b * nb + i * step_chunks + skip, step_chunks - skip)
    seams = [q * nb * W for q in range(T + 1)]
    both = jnp.concatenate(
        [
            jnp.concatenate([white_ref[:, q:q + W] for q in seams], axis=1),
            jnp.concatenate([white_ref[:, q + W:q + 2 * W] for q in seams], axis=1),
        ],
        axis=0,
    )
    acc_ref[...] += nt(jnp.concatenate([gref[:, q:q + W] for q in seams], axis=1), both)

    span = step_len * W
    for step in range(STEPS):
        at, to = step * span, step * step_len * LAGS
        out_ref[to:to + span, :] = acc_ref[at:at + span, 0:W] * scale
        out_ref[to + span:to + 2 * span, :] = acc_ref[at:at + span, W:2 * W] * scale
        extra = main + step * step_len
        out_ref[to + 2 * span:to + 2 * span + step_len, :] = (
            acc_ref[extra:extra + step_len, W:2 * W] * scale
        )

    @pl.when(t < T - 1)
    def _():
        to_right.wait_send()

    @pl.when(t > 0)
    def _():
        to_left.wait_send()

    each(T * half, lambda k: first(k, False))
    each(C - 1, lambda d: second(d).wait_send())
    for d in range(1, T):
        for i in range(PIECES):
            bulk(d, i).wait_send()


def per_device(C, T, raw_strain, fir_taps, sources):
    rows, raw_len = raw_strain.shape
    dec_len = raw_len // DECIM
    nb = dec_len // W
    half = nb * C // (T * nb)
    step_len = sources.shape[1] // T
    ns = STEPS * step_len
    total = T * dec_len
    bf, f32 = jnp.bfloat16, jnp.float32
    flat = pl.pallas_call(
        functools.partial(kernel, C, T, 1.0 / math.sqrt(total)),
        out_shape=pltpu.VMEM((STEPS * LAGS * step_len, rows), f32),
        in_specs=[
            pl.BlockSpec(memory_space=pltpu.HBM),
            pl.BlockSpec(memory_space=pltpu.HBM),
            pl.BlockSpec(memory_space=pltpu.HBM),
        ],
        out_specs=pl.BlockSpec(memory_space=pltpu.VMEM),
        scratch_shapes=[
            pltpu.VMEM((1, TAPS), bf),
            pltpu.SMEM(sources.shape, jnp.int32),
            pltpu.VMEM((T * SLAB, raw_len + (2 * DECIM + 1) * W), bf),
            pltpu.VMEM((2 * STEPS * 16, C * W), bf),
            pltpu.VMEM((rows, LEFT + raw_len + RIGHT), bf),
            pltpu.VMEM((rows, dec_len), f32),
            pltpu.VMEM((rows, dec_len + 2 * W), bf),
            pltpu.VMEM((rows, dec_len + 2 * W), bf),
            pltpu.VMEM((rows, total + 2 * W), bf),
            pltpu.VMEM((T * half + 1, 16, W), bf),
            pltpu.VMEM((C, 16, W), bf),
            pltpu.VMEM((C, 16, W), bf),
            pltpu.VMEM((ns * W + 16, total + W), bf),
            pltpu.VMEM((ns * W + 16, 2 * W), f32),
            pltpu.SemaphoreType.DMA((2,)),
            pltpu.SemaphoreType.DMA((PIECES,)),
            pltpu.SemaphoreType.DMA((2,)),
            pltpu.SemaphoreType.DMA((2,)),
            pltpu.SemaphoreType.DMA((T * half,)),
            pltpu.SemaphoreType.DMA,
            pltpu.SemaphoreType.DMA((C,)),
            pltpu.SemaphoreType.DMA,
            pltpu.SemaphoreType.DMA,
            pltpu.SemaphoreType.DMA((T, PIECES)),
            pltpu.SemaphoreType.DMA((T, PIECES)),
        ],
        compiler_params=pltpu.CompilerParams(
            collective_id=0, has_side_effects=True, vmem_limit_bytes=62 * 1024 * 1024
        ),
    )(raw_strain, fir_taps.reshape(1, TAPS), sources)
    return jnp.swapaxes(flat.reshape(STEPS, LAGS, step_len, rows), 1, 2)


def solution(mesh):
    C, T = mesh.shape["chan"], mesh.shape["tm"]
    return jax.shard_map(
        functools.partial(per_device, C, T),
        mesh=mesh,
        in_specs=(P("chan", "tm"), P(), P()),
        out_specs=P(None, "tm", None, "chan"),
        check_vma=False,
    )
```
